128 devices in a mesh: dp: 16 (over z, x_hi, core), tensor: 8 (over y, x_lo).
Axes of the slice: x: 4 (x_hi: 2, x_lo: 2; x = x_hi * 2 + x_lo), y: 4, z: 4, core: 2. Of those that a mesh axis runs over, the one named last changes fastest.
Arguments:
- tokens: bfloat16 [16384, 5120], P(('dp', 'tensor')), may hold values from -6 to 6
- lengths: int32 [16], P('dp'), may hold values from 128 to 1024, as said below
- attn_gain: float32 [5120], replicated, may hold values from 0.5 to 1.5
- q_gain: float32 [128], replicated, may hold values from 0.8 to 20
- key_norm_gain: float32 [128], replicated, may hold values from 0.8 to 20
- wq_param: float32 [5120, 8192], P('dp', 'tensor'), may hold values from -0.078125 to 0.078125
- wq_moment: float32 [5120, 8192], P('dp', 'tensor'), may hold values from -4 to 4
- wq_second: float32 [5120, 8192], P('dp', 'tensor'), may hold values from 0.01 to 4
- wq_grad: float32 [5120, 8192], P('dp', 'tensor'), may hold values from -6 to 6
- key_weight_matrix: float32 [5120, 1024], P('dp', 'tensor'), may hold values from -0.078125 to 0.078125
- key_weight_first_moment: float32 [5120, 1024], P('dp', 'tensor'), may hold values from -4 to 4
- key_weight_second_moment: float32 [5120, 1024], P('dp', 'tensor'), may hold values from 0.01 to 4
- key_weight_gradient: float32 [5120, 1024], P('dp', 'tensor'), may hold values from -6 to 6
- value_weight_matrix: float32 [5120, 1024], P('dp', 'tensor'), may hold values from -0.078125 to 0.078125
- value_weight_first_moment: float32 [5120, 1024], P('dp', 'tensor'), may hold values from -4 to 4
- value_weight_second_moment: float32 [5120, 1024], P('dp', 'tensor'), may hold values from 0.01 to 4
- value_weight_gradient: float32 [5120, 1024], P('dp', 'tensor'), may hold values from -6 to 6
- wo_param: float32 [5120, 8192], P('dp', 'tensor'), may hold values from -0.0625 to 0.0625
- wo_moment: float32 [5120, 8192], P('dp', 'tensor'), may hold values from -4 to 4
- wo_second: float32 [5120, 8192], P('dp', 'tensor'), may hold values from 0.01 to 4
- wo_grad: float32 [5120, 8192], P('dp', 'tensor'), may hold values from -6 to 6
Outputs:
- attended: bfloat16 [16384, 5120], P(('dp', 'tensor'))
- wq_param_new: float32 [5120, 8192], P('dp', 'tensor')
- wq_moment_new: float32 [5120, 8192], P('dp', 'tensor')
- wq_second_new: float32 [5120, 8192], P('dp', 'tensor')
- wk_param_new: float32 [5120, 1024], P('dp', 'tensor')
- wk_moment_new: float32 [5120, 1024], P('dp', 'tensor')
- wk_second_new: float32 [5120, 1024], P('dp', 'tensor')
- wv_param_new: float32 [5120, 1024], P('dp', 'tensor')
- wv_moment_new: float32 [5120, 1024], P('dp', 'tensor')
- wv_second_new: float32 [5120, 1024], P('dp', 'tensor')
- wo_param_new: float32 [5120, 8192], P('dp', 'tensor')
- wo_moment_new: float32 [5120, 8192], P('dp', 'tensor')
- wo_second_new: float32 [5120, 8192], P('dp', 'tensor')
The draws below stay inside these ranges and needn't reach their ends.
Inputs may be any that keep to these rules, and one draw needn't show every extreme that they name: Positions of prompt p at or past lengths[p] are padding; in every draw some prompt is full.
All inputs are finite; a program needn't handle non-finite values.
Results may differ from the reference program's by a relative error of at most 0.019.
The reference program's roundings to bfloat16 on the way count: a program that leaves them out, or rounds other values in their place, can miss the bound.
Values may be sent and summed in bfloat16 or wider, within the bound.
No kernel may reach another device: no remote copies, remote signals or barrier semaphores. Data moves between devices by JAX's collectives and lax.ppermute only.
A program may use at most 192 MiB of HBM per device.

```python
import math
import jax
import jax.numpy as jnp
from jax import lax

MODEL_WIDTH = 5120
HQ = 64
KEY_VALUE_HEADS = 8
HEAD_SIZE = 128
PROMPT_LENGTH = 1024
STEP = 10
PROMPTS = 16
TOKENS = 16384
N_DP = 16
N_TENSOR = 8


def draw_q_gain(key, part):
    key = jax.random.fold_in(key, 11)
    base = jax.random.uniform(key, (HEAD_SIZE,), jnp.float32, 0.8, 1.2)
    return base


def draw_key_norm_gain(key, part):
    key = jax.random.fold_in(key, 23)
    base = jax.random.uniform(key, (HEAD_SIZE,), jnp.float32, 0.8, 1.2)
    return base


def draw_lengths(key, part):
    key = jax.random.fold_in(key, 7)
    values = jax.random.randint(key, (PROMPTS,), PROMPT_LENGTH // 8, PROMPT_LENGTH + 1)
    full_one = jax.random.randint(jax.random.fold_in(key, 1), (), 0, PROMPTS)
    return jnp.where(jnp.arange(PROMPTS, dtype=jnp.int32) == full_one, PROMPT_LENGTH, values).astype(jnp.int32)


def block_scale(own_key, shape, split, low, high):
    loudness = 1.0
    for dim, parts in split:
        steps = jax.random.uniform(jax.random.fold_in(jax.random.fold_in(own_key, 6), dim), (parts,), jnp.float32, low / len(split), high / len(split))
        loudness = loudness * jnp.repeat(jnp.exp(steps), shape[dim] // parts).reshape((-1,) + (1,) * (len(shape) - 1 - dim))
    return loudness


def noise(rng, shape, scale, bound, cuts=(), kind=jnp.bfloat16):
    array = jax.random.normal(rng, shape, jnp.float32) * scale
    if len(cuts) > 0:
        array = block_scale(rng, shape, cuts, -0.22, 0.18) * array
    return jnp.clip(array, min=-bound, max=bound).astype(kind)


def setup_inputs(seed: int = 0) -> dict:
    key_of = jax.random.split(jax.random.key(seed), 22)
    tokens = noise(key_of[0], (TOKENS, MODEL_WIDTH), 1.0, 6.0, ((0, 128),))
    lengths = draw_lengths(jax.random.fold_in(key_of[21], 71), 0)
    attn_gain = jnp.clip(1.0 + 0.1 * jax.random.normal(key_of[2], (MODEL_WIDTH,), jnp.float32), 0.5, 1.5)
    q_gain = draw_q_gain(jax.random.fold_in(key_of[21], 71), 0)
    key_norm_gain = draw_key_norm_gain(jax.random.fold_in(key_of[21], 71), 0)
    wq_param = noise(key_of[5], (MODEL_WIDTH, HQ * HEAD_SIZE), MODEL_WIDTH ** -0.5, 0.078125, ((0, 16), (1, 8)), jnp.float32)
    wq_moment = noise(key_of[6], (MODEL_WIDTH, HQ * HEAD_SIZE), 0.3, 4.0, ((0, 16), (1, 8)), jnp.float32)
    wq_second = jnp.clip(jnp.exp(math.log(4.0) - 5.9914646 * jax.random.uniform(key_of[7], (MODEL_WIDTH, HQ * HEAD_SIZE), jnp.float32) ** block_scale(key_of[7], (MODEL_WIDTH, HQ * HEAD_SIZE), ((0, 16), (1, 8)), -0.2, 0.2)), 0.01, 4.0)
    wq_grad = noise(key_of[8], (MODEL_WIDTH, HQ * HEAD_SIZE), 1.0, 6.0, ((0, 16), (1, 8)), jnp.float32)
    key_weight_matrix = noise(key_of[9], (MODEL_WIDTH, KEY_VALUE_HEADS * HEAD_SIZE), MODEL_WIDTH ** -0.5, 0.078125, ((0, 16), (1, 8)), jnp.float32)
    key_weight_first_moment = noise(key_of[10], (MODEL_WIDTH, KEY_VALUE_HEADS * HEAD_SIZE), 0.3, 4.0, ((0, 16), (1, 8)), jnp.float32)
    key_weight_second_moment = jnp.clip(jnp.exp(math.log(4.0) - 5.9914646 * jax.random.uniform(key_of[11], (MODEL_WIDTH, KEY_VALUE_HEADS * HEAD_SIZE), jnp.float32) ** block_scale(key_of[11], (MODEL_WIDTH, KEY_VALUE_HEADS * HEAD_SIZE), ((0, 16), (1, 8)), -0.2, 0.2)), 0.01, 4.0)
    key_weight_gradient = noise(key_of[12], (MODEL_WIDTH, KEY_VALUE_HEADS * HEAD_SIZE), 1.0, 6.0, ((0, 16), (1, 8)), jnp.float32)
    value_weight_matrix = noise(key_of[13], (MODEL_WIDTH, KEY_VALUE_HEADS * HEAD_SIZE), MODEL_WIDTH ** -0.5, 0.078125, ((0, 16), (1, 8)), jnp.float32)
    value_weight_first_moment = noise(key_of[14], (MODEL_WIDTH, KEY_VALUE_HEADS * HEAD_SIZE), 0.3, 4.0, ((0, 16), (1, 8)), jnp.float32)
    value_weight_second_moment = jnp.clip(jnp.exp(math.log(4.0) - 5.9914646 * jax.random.uniform(key_of[15], (MODEL_WIDTH, KEY_VALUE_HEADS * HEAD_SIZE), jnp.float32) ** block_scale(key_of[15], (MODEL_WIDTH, KEY_VALUE_HEADS * HEAD_SIZE), ((0, 16), (1, 8)), -0.2, 0.2)), 0.01, 4.0)
    value_weight_gradient = noise(key_of[16], (MODEL_WIDTH, KEY_VALUE_HEADS * HEAD_SIZE), 1.0, 6.0, ((0, 16), (1, 8)), jnp.float32)
    wo_param = noise(key_of[17], (MODEL_WIDTH, HQ * HEAD_SIZE), (HQ * HEAD_SIZE) ** -0.5, 0.0625, ((0, 16), (1, 8)), jnp.float32)
    wo_moment = noise(key_of[18], (MODEL_WIDTH, HQ * HEAD_SIZE), 0.3, 4.0, ((0, 16), (1, 8)), jnp.float32)
    wo_second = jnp.clip(jnp.exp(math.log(4.0) - 5.9914646 * jax.random.uniform(key_of[19], (MODEL_WIDTH, HQ * HEAD_SIZE), jnp.float32) ** block_scale(key_of[19], (MODEL_WIDTH, HQ * HEAD_SIZE), ((0, 16), (1, 8)), -0.2, 0.2)), 0.01, 4.0)
    wo_grad = noise(key_of[20], (MODEL_WIDTH, HQ * HEAD_SIZE), 1.0, 6.0, ((0, 16), (1, 8)), jnp.float32)
    return {"tokens": tokens, "lengths": lengths, "attn_gain": attn_gain, "q_gain": q_gain, "key_norm_gain": key_norm_gain, "wq_param": wq_param, "wq_moment": wq_moment, "wq_second": wq_second, "wq_grad": wq_grad, "key_weight_matrix": key_weight_matrix, "key_weight_first_moment": key_weight_first_moment, "key_weight_second_moment": key_weight_second_moment, "key_weight_gradient": key_weight_gradient, "value_weight_matrix": value_weight_matrix, "value_weight_first_moment": value_weight_first_moment, "value_weight_second_moment": value_weight_second_moment, "value_weight_gradient": value_weight_gradient, "wo_param": wo_param, "wo_moment": wo_moment, "wo_second": wo_second, "wo_grad": wo_grad}


BETA_ONE = 0.9
BETA_TWO = 0.999
ADAM_EPS = 1e-08
LEARN_RATE = 0.0001
DECAY_RATE = 0.01
NORM_EPS = 1e-06
ROPE_BASE = 1000000.0

def adamw_step(current, moment, second, gradient):
    moment_new = BETA_ONE * moment + (1.0 - BETA_ONE) * gradient
    second_new = BETA_TWO * second + (1.0 - BETA_TWO) * gradient * gradient
    moment_hat = moment_new / (1.0 - BETA_ONE ** STEP)
    second_hat = second_new / (1.0 - BETA_TWO ** STEP)
    updated = current - LEARN_RATE * (moment_hat / (jnp.sqrt(second_hat) + ADAM_EPS) + DECAY_RATE * current)
    return (updated, moment_new, second_new)

def root_mean_scale(values, gain):
    mean_sq = lax.optimization_barrier(jnp.mean(values * values, axis=-1, keepdims=True))
    return values * lax.rsqrt(mean_sq + NORM_EPS) * gain

def rope_tables(count, width):
    places = jnp.arange(count, dtype=jnp.float32)
    freqs = ROPE_BASE ** (-jnp.arange(0, width, 2, dtype=jnp.float32) / width)
    angles = places[:, None] * freqs[None, :]
    angles = jnp.concatenate([angles, angles], axis=-1)
    return (jnp.cos(angles), jnp.sin(angles))

def rotate_positions(values, cosine_table, sine_values):
    half = values.shape[-1] // 2
    turned = jnp.concatenate([-values[..., half:], values[..., :half]], axis=-1)
    return values * cosine_table[:, None, :] + turned * sine_values[:, None, :]

def attend(query_rows, key_row_block, value_row_block, length):
    count = query_rows.shape[0]
    heads = query_rows.shape[1]
    groups = key_row_block.shape[1]
    share = heads // groups
    grouped = query_rows.reshape(count, groups, share, HEAD_SIZE).transpose(1, 2, 0, 3)
    keys_first = key_row_block.transpose(1, 0, 2)
    values_first = value_row_block.transpose(1, 0, 2)
    places = jnp.arange(count, dtype=jnp.int32)
    visible = (places[None, :] <= places[:, None]) & (places[None, :] < length)

    def one_group(items):
        q_block, k_block, v_block = items
        scores = jnp.einsum('gsd,td->gst', q_block.astype(jnp.float32), k_block.astype(jnp.float32)) / math.sqrt(HEAD_SIZE)
        masked = jnp.where(visible[None], scores, -1e+30)
        maxima = lax.optimization_barrier(jnp.max(masked, axis=-1, keepdims=True))
        exps = jnp.where(visible[None], jnp.exp(masked - maxima), 0.0)
        totals = lax.optimization_barrier(jnp.sum(exps, axis=-1, keepdims=True))
        probs = (exps / totals).astype(jnp.bfloat16)
        mixed = jnp.einsum('gst,td->gsd', probs.astype(jnp.float32), v_block.astype(jnp.float32))
        return mixed.astype(jnp.bfloat16)
    context = lax.map(one_group, (grouped, keys_first, values_first))
    return context.transpose(2, 0, 1, 3).reshape(count, heads * HEAD_SIZE)

def reference(tokens, lengths, attn_gain, q_gain, key_norm_gain, wq_param, wq_moment, wq_second, wq_grad, key_weight_matrix, key_weight_first_moment, key_weight_second_moment, key_weight_gradient, value_weight_matrix, value_weight_first_moment, value_weight_second_moment, value_weight_gradient, wo_param, wo_moment, wo_second, wo_grad):
    new_q = adamw_step(wq_param, wq_moment, wq_second, wq_grad)
    new_k = adamw_step(key_weight_matrix, key_weight_first_moment, key_weight_second_moment, key_weight_gradient)
    new_v = adamw_step(value_weight_matrix, value_weight_first_moment, value_weight_second_moment, value_weight_gradient)
    new_o = adamw_step(wo_param, wo_moment, wo_second, wo_grad)
    rollout_q = new_q[0].astype(jnp.bfloat16)
    rollout_k = new_k[0].astype(jnp.bfloat16)
    rollout_v = new_v[0].astype(jnp.bfloat16)
    rollout_o = new_o[0].astype(jnp.bfloat16)
    cosine_table, sine_values = rope_tables(PROMPT_LENGTH, HEAD_SIZE)
    out_parts = rollout_o.reshape(MODEL_WIDTH, N_TENSOR, -1).astype(jnp.float32)

    def prompt_block(items):
        own_rows, length = items
        normed = root_mean_scale(own_rows.astype(jnp.float32), attn_gain).astype(jnp.bfloat16)
        query_flat = jnp.dot(normed, rollout_q, preferred_element_type=jnp.float32)
        key_flattened = jnp.dot(normed, rollout_k, preferred_element_type=jnp.float32)
        value_flattened = jnp.dot(normed, rollout_v, preferred_element_type=jnp.float32)
        query_rows = rotate_positions(root_mean_scale(query_flat.reshape(PROMPT_LENGTH, HQ, HEAD_SIZE), q_gain), cosine_table, sine_values).astype(jnp.bfloat16)
        key_row_block = rotate_positions(root_mean_scale(key_flattened.reshape(PROMPT_LENGTH, KEY_VALUE_HEADS, HEAD_SIZE), key_norm_gain), cosine_table, sine_values).astype(jnp.bfloat16)
        value_row_block = value_flattened.astype(jnp.bfloat16).reshape(PROMPT_LENGTH, KEY_VALUE_HEADS, HEAD_SIZE)
        context = attend(query_rows, key_row_block, value_row_block, length)
        pieces = context.reshape(PROMPT_LENGTH, N_TENSOR, -1).astype(jnp.float32)
        partials = jnp.einsum('snc,dnc->nsd', pieces, out_parts)
        rounded = lax.optimization_barrier(partials.astype(jnp.bfloat16))
        summed = lax.optimization_barrier(jnp.sum(rounded.astype(jnp.float32), axis=0))
        return summed.astype(jnp.bfloat16)
    attended = lax.map(prompt_block, (tokens.reshape(N_DP, PROMPT_LENGTH, MODEL_WIDTH), lengths))
    attended = attended.reshape(N_DP * PROMPT_LENGTH, MODEL_WIDTH)
    return (attended, new_q[0], new_q[1], new_q[2], new_k[0], new_k[1], new_k[2], new_v[0], new_v[1], new_v[2], new_o[0], new_o[1], new_o[2])
```

```python
import functools
import itertools
import math

import jax
import jax.numpy as jnp
from jax import lax
from jax.experimental import pallas as pl
from jax.experimental.pallas import tpu as pltpu
from jax.sharding import Mesh
from jax.sharding import PartitionSpec as P

HEAD_SIZE = 128
STEP = 10

BETA_ONE = 0.9
BETA_TWO = 0.999
ADAM_EPS = 1e-08
LEARN_RATE = 0.0001
DECAY_RATE = 0.01
NORM_EPS = 1e-06
ROPE_BASE = 1000000.0

AXES = ("z", "xh", "c", "y", "xl")
SIZES = dict(z=4, xh=2, c=2, y=4, xl=2)
WIDTH = 5120
BLOCK = 128
OWN = 512
BF16 = jnp.bfloat16
F32 = jnp.float32


def adamw_step(current, moment, second, gradient):
    moment_new = BETA_ONE * moment + (1.0 - BETA_ONE) * gradient
    second_new = BETA_TWO * second + (1.0 - BETA_TWO) * gradient * gradient
    moment_hat = moment_new / (1.0 - BETA_ONE**STEP)
    second_hat = second_new / (1.0 - BETA_TWO**STEP)
    updated = current - LEARN_RATE * (
        moment_hat / (jnp.sqrt(second_hat) + ADAM_EPS) + DECAY_RATE * current
    )
    return (updated, moment_new, second_new)


def root_mean_scale(values, gain):
    mean_sq = jnp.mean(values * values, axis=-1, keepdims=True)
    return values * lax.rsqrt(mean_sq + NORM_EPS) * gain


def permute(axes, move):
    axes = tuple(a for a in AXES if a in axes)
    places = list(itertools.product(*[range(SIZES[a]) for a in axes]))
    index = {place: i for i, place in enumerate(places)}
    pairs = []
    for place in places:
        there = move(dict(zip(axes, place)))
        pairs.append((index[place], index[tuple(there[a] for a in axes)]))
    return lambda v: lax.ppermute(v, axes, pairs)


def ring_move(axis):
    def move(place):
        step = 1 if place["c"] == 0 else -1
        if axis == "x":
            x = (place["xh"] * 2 + place["xl"] + step) % 4
            place["xh"], place["xl"] = x // 2, x % 2
        else:
            place[axis] = (place[axis] + step) % SIZES[axis]
        return place

    return move


def swap_move(axis):
    def move(place):
        place[axis] = 1 - place[axis]
        return place

    return move


ring_y = permute(("y", "c"), ring_move("y"))
swap_xl = permute(("xl",), swap_move("xl"))


def position_tables(xl):
    block = jnp.arange(4, dtype=jnp.int32)[:, None] * 2 + xl
    places = (block * BLOCK + jnp.arange(BLOCK, dtype=jnp.int32)[None, :]).reshape(-1)
    freqs = ROPE_BASE ** (-jnp.arange(0, HEAD_SIZE, 2, dtype=F32) / HEAD_SIZE)
    angles = places.astype(F32)[:, None] * freqs[None, :]
    cosine, sine = jnp.cos(angles), jnp.sin(angles)
    return (
        jnp.concatenate([cosine, cosine], axis=-1),
        jnp.concatenate([-sine, sine], axis=-1),
    )


def norm_rope(u, gain, cosine, sine):
    mean_sq = jnp.mean(u * u, axis=-1, keepdims=True)
    u = u * lax.rsqrt(mean_sq + NORM_EPS) * gain
    return u * cosine + pltpu.roll(u, HEAD_SIZE // 2, 1) * sine


def qkv_kernel(x_ref, w_ref, cos_ref, sin_ref, qg_ref, kg_ref, q_ref, kv_ref, acc):
    step = pl.program_id(1)
    last = pl.num_programs(1) - 1
    rows = x_ref[...]
    for n in range(0, 1280, 256):
        part = w_ref[0, :, 0, :, :, n : n + 256].reshape(1280, 256)
        out = jnp.dot(rows, part, preferred_element_type=F32)

        @pl.when(step == 0)
        def _():
            acc[:, n : n + 256] = out

        @pl.when(step > 0)
        def _():
            acc[:, n : n + 256] += out

    @pl.when(step == last)
    def _():
        cosine, sine = cos_ref[...], sin_ref[...]
        for h in range(8):
            u = acc[:, h * 128 : (h + 1) * 128]
            q_ref[0, :, h * 128 : (h + 1) * 128] = norm_rope(u, qg_ref[...], cosine, sine).astype(BF16)
        kv_ref[0, :, :128] = norm_rope(acc[:, 1024:1152], kg_ref[...], cosine, sine).astype(BF16)
        kv_ref[0, :, 128:] = acc[:, 1152:1280].astype(BF16)


def qkv_project(rows, weights, cosine, sine, q_gain, k_gain):
    whole = lambda shape: pl.BlockSpec(shape, lambda g, s: (0,) * len(shape))
    return pl.pallas_call(
        qkv_kernel,
        grid=(2, 4),
        in_specs=[
            pl.BlockSpec((OWN, 1280), lambda g, s: (0, s)),
            pl.BlockSpec((1, 2, 1, 2, 320, 1280), lambda g, s: (s, 0, g, 0, 0, 0)),
            whole((OWN, 128)),
            whole((OWN, 128)),
            whole((1, 128)),
            whole((1, 128)),
        ],
        out_specs=[
            pl.BlockSpec((1, OWN, 1024), lambda g, s: (g, 0, 0)),
            pl.BlockSpec((1, OWN, 256), lambda g, s: (g, 0, 0)),
        ],
        out_shape=[
            jax.ShapeDtypeStruct((2, OWN, 1024), BF16),
            jax.ShapeDtypeStruct((2, OWN, 256), BF16),
        ],
        scratch_shapes=[pltpu.VMEM((OWN, 1280), F32)],
        compiler_params=pltpu.CompilerParams(vmem_limit_bytes=48 << 20),
        cost_estimate=pl.CostEstimate(flops=2 * 512 * 5120 * 2560, bytes_accessed=40 << 20, transcendentals=0),
        name="qkv",
    )(rows, weights, cosine, sine, q_gain, k_gain)


SCALE = math.log2(math.e) / math.sqrt(HEAD_SIZE)


def attend_kernel(info_ref, q_ref, own_ref, far_ref, o_ref):
    length, xl = info_ref[0], info_ref[1]
    block = pl.program_id(1)

    def body(j):
        n = (j + 1) * BLOCK
        keys = jnp.concatenate([own_ref[0, :n, :128], far_ref[0, :n, :128]], axis=0)
        values = jnp.concatenate([own_ref[0, :n, 128:], far_ref[0, :n, 128:]], axis=0)
        row = lax.broadcasted_iota(jnp.int32, (BLOCK, 2 * n), 0)
        col = lax.broadcasted_iota(jnp.int32, (BLOCK, 2 * n), 1)
        own = col < n
        inner = jnp.where(own, col, col - n)
        side = jnp.where(own, xl, 1 - xl)
        place = (inner // BLOCK * 2 + side) * BLOCK + inner % BLOCK
        query = (2 * j + xl) * BLOCK + row
        bias = jnp.where((place <= query) & (place < length), 0.0, -1e30).astype(F32)
        for h in range(8):
            lanes = slice(h * 128, (h + 1) * 128)
            scores = lax.dot_general(
                q_ref[0, :, lanes], keys, (((1,), (1,)), ((), ())), preferred_element_type=F32
            )
            scores = scores + bias
            top = jnp.max(scores, axis=-1, keepdims=True)
            exps = jnp.exp2((scores - top) * SCALE)
            total = jnp.sum(exps, axis=-1, keepdims=True)
            mixed = jnp.dot(exps.astype(BF16), values, preferred_element_type=F32)
            o_ref[0, :, lanes] = (mixed / total).astype(BF16)

    for j in range(4):
        pl.when(block == j)(functools.partial(body, j))


def attend(info, queries, own, far):
    return pl.pallas_call(
        attend_kernel,
        grid=(2, 4),
        in_specs=[
            pl.BlockSpec(memory_space=pltpu.SMEM),
            pl.BlockSpec((1, BLOCK, 1024), lambda g, j: (g, j, 0)),
            pl.BlockSpec((1, OWN, 256), lambda g, j: (g, 0, 0)),
            pl.BlockSpec((1, OWN, 256), lambda g, j: (g, 0, 0)),
        ],
        out_specs=pl.BlockSpec((1, BLOCK, 1024), lambda g, j: (g, j, 0)),
        out_shape=jax.ShapeDtypeStruct((2, OWN, 1024), BF16),
        compiler_params=pltpu.CompilerParams(vmem_limit_bytes=48 << 20),
        cost_estimate=pl.CostEstimate(flops=6 << 30, bytes_accessed=5 << 20, transcendentals=5 << 20),
        name="attend",
    )(info, queries, own, far)


def out_kernel(ctx_ref, w_ref, o_ref):
    for f in range(4):
        total = None
        for g in range(2):
            part = lax.dot_general(
                ctx_ref[g],
                w_ref[0, f // 2, g, f % 2],
                (((1,), (1,)), ((), ())),
                preferred_element_type=F32,
            )
            total = part if total is None else total + part
        o_ref[:, f * 320 : (f + 1) * 320] = total.astype(BF16)


def out_project(context, weights, first, count):
    return pl.pallas_call(
        out_kernel,
        grid=(count,),
        in_specs=[
            pl.BlockSpec((2, OWN, 1024), lambda s: (0, 0, 0)),
            pl.BlockSpec((1, 2, 2, 2, 320, 1024), lambda s: (s + first, 0, 0, 0, 0, 0)),
        ],
        out_specs=pl.BlockSpec((OWN, 1280), lambda s: (0, s)),
        out_shape=jax.ShapeDtypeStruct((OWN, 1280 * count), BF16),
        compiler_params=pltpu.CompilerParams(vmem_limit_bytes=48 << 20),
        cost_estimate=pl.CostEstimate(
            flops=2 * 512 * 2048 * 1280 * count, bytes_accessed=count * (7 << 20), transcendentals=0
        ),
        name="out_project",
    )(context, weights)


def scatter_sum(partial, y, core):
    blocks = partial.reshape(4, BLOCK, -1)
    step = 1 - 2 * core

    def own(back):
        return lax.dynamic_index_in_dim(blocks, jnp.mod(y - step * back, 4), 0, keepdims=False)

    moving = own(1)
    for s in range(1, 4):
        arrived = ring_y(moving)
        moving = (arrived.astype(F32) + own(s + 1).astype(F32)).astype(BF16)
    return moving


def gather_tokens(mine, y, core):
    step = 1 - 2 * core
    whole = jnp.zeros((4, BLOCK, WIDTH), BF16)
    moving = mine
    for s in range(4):
        whole = lax.dynamic_update_index_in_dim(whole, moving, jnp.mod(y - step * s, 4), 0)
        if s < 3:
            moving = ring_y(moving)
    return whole.reshape(OWN, WIDTH)


def gather_weights(shard):
    whole = lax.all_gather(shard, ("z", "xh", "xl", "c"), axis=0, tiled=False)
    return whole.reshape((4, 2, 2, 2) + shard.shape)


def local(
    tokens,
    lengths,
    attn_gain,
    q_gain,
    key_norm_gain,
    wq_param,
    wq_moment,
    wq_second,
    wq_grad,
    key_weight_matrix,
    key_weight_first_moment,
    key_weight_second_moment,
    key_weight_gradient,
    value_weight_matrix,
    value_weight_first_moment,
    value_weight_second_moment,
    value_weight_gradient,
    wo_param,
    wo_moment,
    wo_second,
    wo_grad,
):
    y, core, xl = lax.axis_index("y"), lax.axis_index("c"), lax.axis_index("xl")
    normed_own = root_mean_scale(tokens.astype(F32), attn_gain).astype(BF16)
    new_k = adamw_step(
        key_weight_matrix, key_weight_first_moment, key_weight_second_moment, key_weight_gradient
    )
    new_v = adamw_step(
        value_weight_matrix,
        value_weight_first_moment,
        value_weight_second_moment,
        value_weight_gradient,
    )
    new_q = adamw_step(wq_param, wq_moment, wq_second, wq_grad)
    new_o = adamw_step(wo_param, wo_moment, wo_second, wo_grad)
    shard_qkv = jnp.concatenate([new_q[0], new_k[0], new_v[0]], axis=1).astype(BF16)
    shard_o = new_o[0].astype(BF16)
    whole_qkv = gather_weights(shard_qkv)
    whole_o = gather_weights(shard_o)
    normed = gather_tokens(normed_own, y, core)
    cosine, sine = position_tables(xl)
    queries, own_kv = qkv_project(
        normed, whole_qkv, cosine, sine, q_gain[None], key_norm_gain[None]
    )
    far_kv = swap_xl(own_kv)
    info = jnp.stack([lengths[0], xl.astype(jnp.int32)])
    context = attend(info, queries, own_kv, far_kv)
    halves = [
        scatter_sum(out_project(context, whole_o, first, 2), y, core) for first in (0, 2)
    ]
    attended = jnp.concatenate(halves, axis=1)
    return (attended,) + new_q + new_k + new_v + new_o


def solution(mesh):
    fine = Mesh(mesh.devices.reshape([SIZES[a] for a in AXES]), AXES)
    dp, tensor = ("z", "xh", "c"), ("y", "xl")
    weight = P(dp, tensor)
    rows = P(dp + tensor, None)
    return jax.shard_map(
        local,
        mesh=fine,
        in_specs=(rows, P(dp), P(), P(), P()) + (weight,) * 16,
        out_specs=(rows,) + (weight,) * 12,
        check_vma=False,
    )
```

```python
import functools
import itertools
import math

import jax
import jax.numpy as jnp
from jax import lax
from jax.experimental import pallas as pl
from jax.experimental.pallas import tpu as pltpu
from jax.sharding import Mesh
from jax.sharding import PartitionSpec as P

HEAD_SIZE = 128
STEP = 10

BETA_ONE = 0.9
BETA_TWO = 0.999
ADAM_EPS = 1e-08
LEARN_RATE = 0.0001
DECAY_RATE = 0.01
NORM_EPS = 1e-06
ROPE_BASE = 1000000.0

AXES = ("z", "xh", "c", "y", "xl")
SIZES = dict(z=4, xh=2, c=2, y=4, xl=2)
WIDTH = 5120
BLOCK = 128
OWN = 512
BF16 = jnp.bfloat16

LIGHT = pl.CostEstimate(flops=1 << 20, bytes_accessed=1 << 10, transcendentals=0)

F32 = jnp.float32


def adamw_step(current, moment, second, gradient):
    moment_new = BETA_ONE * moment + (1.0 - BETA_ONE) * gradient
    second_new = BETA_TWO * second + (1.0 - BETA_TWO) * gradient * gradient
    moment_hat = moment_new / (1.0 - BETA_ONE**STEP)
    second_hat = second_new / (1.0 - BETA_TWO**STEP)
    updated = current - LEARN_RATE * (
        moment_hat / (jnp.sqrt(second_hat) + ADAM_EPS) + DECAY_RATE * current
    )
    return (updated, moment_new, second_new)


def root_mean_scale(values, gain):
    mean_sq = jnp.mean(values * values, axis=-1, keepdims=True)
    return values * lax.rsqrt(mean_sq + NORM_EPS) * gain


def permute(axes, move):
    axes = tuple(a for a in AXES if a in axes)
    places = list(itertools.product(*[range(SIZES[a]) for a in axes]))
    index = {place: i for i, place in enumerate(places)}
    pairs = []
    for place in places:
        there = move(dict(zip(axes, place)))
        pairs.append((index[place], index[tuple(there[a] for a in axes)]))
    return lambda v: lax.ppermute(v, axes, pairs)


def ring_move(axis, places=1):
    def move(place):
        step = places if place["c"] == 0 else -places
        if axis == "x":
            x = (place["xh"] * 2 + place["xl"] + step) % 4
            place["xh"], place["xl"] = x // 2, x % 2
        else:
            place[axis] = (place[axis] + step) % SIZES[axis]
        return place

    return move


def swap_move(axis):
    def move(place):
        place[axis] = 1 - place[axis]
        return place

    return move


ring_y = permute(("y", "c"), ring_move("y"))
ring_z = permute(("z", "c"), ring_move("z"))
ring_x = permute(("xh", "xl", "c"), ring_move("x"))
direct_y = {n: permute(("y", "c"), ring_move("y", n)) for n in (1, 2, 3)}
swap_xl = permute(("xl",), swap_move("xl"))
swap_core = permute(("c",), swap_move("c"))


def position_tables(xl):
    block = jnp.arange(4, dtype=jnp.int32)[:, None] * 2 + xl
    places = (block * BLOCK + jnp.arange(BLOCK, dtype=jnp.int32)[None, :]).reshape(-1)
    freqs = ROPE_BASE ** (-jnp.arange(0, HEAD_SIZE, 2, dtype=F32) / HEAD_SIZE)
    angles = places.astype(F32)[:, None] * freqs[None, :]
    cosine, sine = jnp.cos(angles), jnp.sin(angles)
    return (
        jnp.concatenate([cosine, cosine], axis=-1),
        jnp.concatenate([-sine, sine], axis=-1),
    )


def norm_rope(u, gain, cosine, sine):
    mean_sq = jnp.mean(u * u, axis=-1, keepdims=True)
    u = u * lax.rsqrt(mean_sq + NORM_EPS) * gain
    return u * cosine + pltpu.roll(u, HEAD_SIZE // 2, 1) * sine


def heads_out(total, refs, gains, cosine, sine):
    for n, ((ref, lanes), gain) in enumerate(zip(refs, gains)):
        u = total[:, n * 128 : (n + 1) * 128]
        ref[0, :, lanes] = (u if gain is None else norm_rope(u, gain, cosine, sine)).astype(BF16)


def lane_block(n):
    return slice(n * 128, (n + 1) * 128)


def kv_kernel(core_ref, x_ref, w_ref, cos_ref, sin_ref, kg_ref, kv_ref, acc):
    step = pl.program_id(0)
    part = w_ref[...].reshape(1280, 256)
    for p in range(2):
        rows = x_ref[p]
        out = jnp.dot(rows, part, preferred_element_type=F32)
        acc[p] = jnp.where(step == 0, out, acc[p] + out)

    @pl.when(step == pl.num_programs(0) - 1)
    def _():
        for p in range(2):
            keys = norm_rope(acc[p, :, :128], kg_ref[...], cos_ref[...], sin_ref[...])
            kv_ref[p, :, :128] = keys.astype(BF16)
            kv_ref[p, :, 128:] = acc[p, :, 128:].astype(BF16)


def key_values(core, rows, weights, cosine, sine, k_gain):
    fixed = lambda shape: pl.BlockSpec(shape, lambda k, s: (0,) * len(shape))
    return pl.pallas_call(
        kv_kernel,
        grid_spec=pltpu.PrefetchScalarGridSpec(
            num_scalar_prefetch=1,
            grid=(4,),
            in_specs=[
                pl.BlockSpec((2, OWN, 1280), lambda k, s: (0, 0, k)),
                pl.BlockSpec((1, 2, 1, 2, 320, 256), lambda k, s: (k, 0, s[0], 0, 0, 4)),
                fixed((OWN, 128)),
                fixed((OWN, 128)),
                fixed((1, 128)),
            ],
            out_specs=fixed((2, OWN, 256)),
            scratch_shapes=[pltpu.VMEM((2, OWN, 256), F32)],
        ),
        out_shape=jax.ShapeDtypeStruct((2, OWN, 256), BF16),
        compiler_params=pltpu.CompilerParams(vmem_limit_bytes=48 << 20),
        cost_estimate=LIGHT,
        name="key_values",
    )(core, rows, weights, cosine, sine, k_gain)


def query_kernel(core_ref, x_ref, w0_ref, w1_ref, cos_ref, sin_ref, qg_ref, q_ref):
    for n in range(4):
        w_ref, lanes = (w0_ref, w1_ref)[n // 2], slice(n % 2 * 256, n % 2 * 256 + 256)
        part = w_ref[:, :, 0, :, :, lanes].reshape(WIDTH, 256)
        out = jnp.dot(x_ref[0], part, preferred_element_type=F32)
        heads_out(
            out,
            [(q_ref, lane_block(2 * n)), (q_ref, lane_block(2 * n + 1))],
            [qg_ref[...]] * 2,
            cos_ref[...],
            sin_ref[...],
        )


def queries_of(core, rows, weights, cosine, sine, q_gain):
    fixed = lambda shape: pl.BlockSpec(shape, lambda p, m, s: (0,) * len(shape))
    weight = lambda half: pl.BlockSpec((4, 2, 1, 2, 320, 512), lambda p, m, s: (0, 0, s[0], 0, 0, half))
    return pl.pallas_call(
        query_kernel,
        grid_spec=pltpu.PrefetchScalarGridSpec(
            num_scalar_prefetch=1,
            grid=(2, 2),
            in_specs=[
                pl.BlockSpec((1, 256, WIDTH), lambda p, m, s: (p, m, 0)),
                weight(0),
                weight(1),
                pl.BlockSpec((256, 128), lambda p, m, s: (m, 0)),
                pl.BlockSpec((256, 128), lambda p, m, s: (m, 0)),
                fixed((1, 128)),
            ],
            out_specs=pl.BlockSpec((1, 256, 1024), lambda p, m, s: (p, m, 0)),
        ),
        out_shape=jax.ShapeDtypeStruct((2, OWN, 1024), BF16),
        compiler_params=pltpu.CompilerParams(vmem_limit_bytes=48 << 20),
        cost_estimate=LIGHT,
        name="queries",
    )(core, rows, weights, weights, cosine, sine, q_gain)


SCALE = math.log2(math.e) / math.sqrt(HEAD_SIZE)


def attend_kernel(info_ref, q_ref, own_ref, far_ref, o_ref):
    prompt, block = pl.program_id(0), pl.program_id(1)
    length, xl = info_ref[prompt], info_ref[2]

    def body(j):
        n = (j + 1) * BLOCK
        keys = jnp.concatenate([own_ref[0, :n, :128], far_ref[0, :n, :128]], axis=0)
        values = jnp.concatenate([own_ref[0, :n, 128:], far_ref[0, :n, 128:]], axis=0)
        values = jnp.concatenate([values, jnp.ones_like(values)], axis=1)
        row = lax.broadcasted_iota(jnp.int32, (BLOCK, 2 * n), 0)
        col = lax.broadcasted_iota(jnp.int32, (BLOCK, 2 * n), 1)
        own = col < n
        inner = jnp.where(own, col, col - n)
        side = jnp.where(own, xl, 1 - xl)
        place = (inner // BLOCK * 2 + side) * BLOCK + inner % BLOCK
        query = (2 * j + xl) * BLOCK + row
        bias = jnp.where((place <= query) & (place < length), 0.0, -1e30).astype(F32)
        for h in range(8):
            rows = q_ref[0, :, lane_block(h)]
            scores = lax.dot_general(rows, keys, (((1,), (1,)), ((), ())), preferred_element_type=F32)
            scores = scores + bias
            top = jnp.max(scores, axis=-1, keepdims=True)
            exps = jnp.exp2((scores - top) * SCALE).astype(BF16)
            mixed = jnp.dot(exps, values, preferred_element_type=F32)
            o_ref[0, :, lane_block(h)] = (mixed[:, :128] / mixed[:, 128:]).astype(BF16)

    for j in range(4):
        pl.when(block == j)(functools.partial(body, j))


def attend(info, queries, own, far):
    whole = pl.BlockSpec((1, OWN, 256), lambda p, j: (p, 0, 0))
    rows = lambda lanes: pl.BlockSpec((1, BLOCK, lanes), lambda p, j: (p, j, 0))
    return pl.pallas_call(
        attend_kernel,
        grid=(2, 4),
        in_specs=[pl.BlockSpec(memory_space=pltpu.SMEM), rows(1024), whole, whole],
        out_specs=rows(1024),
        out_shape=jax.ShapeDtypeStruct((2, OWN, 1024), BF16),
        compiler_params=pltpu.CompilerParams(vmem_limit_bytes=40 << 20),
        cost_estimate=LIGHT,
        name="attend",
    )(info, queries, own, far)


def out_kernel(info_ref, ctx_ref, a0_ref, a1_ref, a2_ref, a3_ref, wb_ref, other_ref, mine_ref):
    turn = info_ref[1 + pl.program_id(0)]
    contract = (((1,), (1,)), ((), ()))
    rows = ctx_ref[0]
    def write(a_ref, ref):
        total = lax.dot_general(
            rows[:, :512], a_ref[...].reshape(1280, 512), contract, preferred_element_type=F32
        )
        total += lax.dot_general(
            rows[:, 512:], wb_ref[...].reshape(1280, 512), contract, preferred_element_type=F32
        )
        ref[...] = total.astype(BF16)

    for n, a_ref in enumerate((a0_ref, a1_ref, a2_ref, a3_ref)):
        for p, ref in enumerate((other_ref, mine_ref)):
            pl.when((turn == n) & (pl.program_id(1) == p))(functools.partial(write, a_ref, ref))


def out_project(context, blocks, half_b, first, at):
    turns = [jnp.mod(at.step * (at.z - first - f), 4) for f in range(2)]
    info = jnp.stack([at.core] + turns).astype(jnp.int32)
    piece = pl.BlockSpec((4, 320, 512), lambda f, p, s: (0, 0, 0))
    out = pl.BlockSpec((OWN, 1280), lambda f, p, s: (0, f))
    return pl.pallas_call(
        out_kernel,
        grid_spec=pltpu.PrefetchScalarGridSpec(
            num_scalar_prefetch=1,
            grid=(2, 2),
            in_specs=[pl.BlockSpec((1, OWN, 1024), lambda f, p, s: ((1 - p) * (1 - s[0]) + p * s[0], 0, 0))]
            + [piece] * 4
            + [pl.BlockSpec((1, 2, 2, 320, 512), lambda f, p, s: (f + first, 0, 0, 0, 0))],
            out_specs=[out, out],
        ),
        out_shape=[jax.ShapeDtypeStruct((OWN, 2560), BF16)] * 2,
        compiler_params=pltpu.CompilerParams(vmem_limit_bytes=48 << 20),
        cost_estimate=LIGHT,
        name="out_project",
    )(info, context, *blocks, half_b)


def after(value, *before):
    return lax.optimization_barrier((value,) + before)[0]


def add_bf16(a, b):
    return (a.astype(F32) + b.astype(F32)).astype(BF16)


def scatter_sum(blocks, y, core):
    step = 1 - 2 * core

    def own(back):
        return lax.dynamic_index_in_dim(blocks, jnp.mod(y - step * back, 4), 0, keepdims=False)

    moving = own(1)
    for s in range(1, 4):
        moving = add_bf16(ring_y(moving), own(s + 1))
    return moving


def gather_tokens(mine, y, core):
    step = 1 - 2 * core
    whole = jnp.zeros((2, 4, BLOCK, WIDTH), BF16)
    for s in range(4):
        here = mine if s == 0 else direct_y[s](mine)
        there = swap_core(here)
        whole = lax.dynamic_update_slice(whole, here[None, None], (core, jnp.mod(y - step * s, 4), 0, 0))
        whole = lax.dynamic_update_slice(whole, there[None, None], (1 - core, jnp.mod(y + step * s, 4), 0, 0))
    return whole.reshape(2, OWN, WIDTH)


def pick(index, options):
    return lax.select_n(index.astype(jnp.int32), *options)


class Place:
    def __init__(self):
        self.x = lax.axis_index("xh") * 2 + lax.axis_index("xl")
        self.z, self.y = lax.axis_index("z"), lax.axis_index("y")
        self.core, self.xl = lax.axis_index("c"), lax.axis_index("xl")
        self.step = 1 - 2 * self.core


def ring_pieces(shard, ring):
    pieces = [shard]
    for _ in range(3):
        pieces.append(ring(pieces[-1]))
    return pieces


def block_of_x(pieces, at):
    from_x = lambda x_there: pick(jnp.mod(at.step * (at.x - x_there), 4), pieces)
    keep = [from_x(at.core), from_x(at.core + 2)]
    got = swap_core(jnp.stack([from_x(1 - at.core), from_x(3 - at.core)]))
    mine = jnp.stack([keep[0], got[0], keep[1], got[1]])
    theirs = jnp.stack([got[0], keep[0], got[1], keep[1]])
    return jnp.where(at.core == 0, mine, theirs)


def lay_out(blocks, at):
    whole = jnp.zeros((4,) + blocks[0].shape, BF16)
    for s, block in enumerate(blocks):
        whole = lax.dynamic_update_index_in_dim(whole, block, jnp.mod(at.z - at.step * s, 4), 0)
    return whole


def place_block(whole, s, blocks, at):
    return lax.dynamic_update_index_in_dim(whole, blocks[s], jnp.mod(at.z - at.step * s, 4), 0)


def place_pair(whole, pair, even_one, odd_one, at):
    odd = jnp.mod(at.x + at.core, 2)
    zero = jnp.int32(0)
    got = swap_core(jnp.where(odd == 0, odd_one, even_one))
    keep = jnp.where(odd == 0, even_one, odd_one)
    for piece, sign, c_there in ((keep, -1, at.core), (got, 1, 1 - at.core)):
        x_there = jnp.mod(at.x + sign * at.step * (odd + pair), 4)
        whole = lax.dynamic_update_slice(
            whole, piece[:, None, None], (zero, x_there // 2, c_there, zero, zero)
        )
    return whole


def local(
    tokens,
    lengths,
    attn_gain,
    q_gain,
    key_norm_gain,
    wq_param,
    wq_moment,
    wq_second,
    wq_grad,
    key_weight_matrix,
    key_weight_first_moment,
    key_weight_second_moment,
    key_weight_gradient,
    value_weight_matrix,
    value_weight_first_moment,
    value_weight_second_moment,
    value_weight_gradient,
    wo_param,
    wo_moment,
    wo_second,
    wo_grad,
):
    at = Place()
    new_k = adamw_step(
        key_weight_matrix, key_weight_first_moment, key_weight_second_moment, key_weight_gradient
    )
    new_v = adamw_step(
        value_weight_matrix,
        value_weight_first_moment,
        value_weight_second_moment,
        value_weight_gradient,
    )
    new_q = adamw_step(wq_param, wq_moment, wq_second, wq_grad)
    shard = jnp.concatenate([new_q[0], new_k[0], new_v[0]], axis=1).astype(BF16)
    whole = lax.all_gather(shard, ("z", "xh", "xl", "c"), axis=0, tiled=False)
    whole = whole.reshape(4, 2, 2, 2, 320, 1280)

    new_o = adamw_step(wo_param, wo_moment, wo_second, after(wo_grad, shard))
    shard_o = new_o[0].astype(BF16)
    normed_own = root_mean_scale(after(tokens, shard).astype(F32), attn_gain).astype(BF16)
    normed = gather_tokens(normed_own, at.y, at.core)
    far_length = swap_core(lengths)
    both = jnp.where(
        at.core == 0, jnp.stack([lengths[0], far_length[0]]), jnp.stack([far_length[0], lengths[0]])
    )
    cosine, sine = position_tables(at.xl)

    oa = ring_pieces(shard_o[:, :512], ring_x)
    ob = ring_pieces(shard_o[:, 512:], ring_z)
    oa, ob = [block_of_x(oa, at)], [lay_out(ob, at)]
    oa += [ring_z(oa[0]), None]
    ob += [ring_x(ob[0]), None]

    group = at.core.astype(jnp.int32)[None]
    empty = jnp.zeros((4, 2, 2, 320, 512), BF16)
    normed, oa[1], ob[1], both, empty = lax.optimization_barrier((normed, oa[1], ob[1], both, empty))
    own_kv = key_values(group, normed, whole, cosine, sine, key_norm_gain[None])
    far_kv = swap_xl(own_kv)
    oa[2], ob[2] = ring_z(oa[1]), ring_x(ob[1])
    done = after((oa[0], oa[1], ob[0], ob[1]), own_kv)
    half_b = place_pair(empty, 0, done[2], done[3], at)
    queries = queries_of(group, after(normed, own_kv), whole, cosine, sine, q_gain[None])
    oa[2], ob[2], queries = after((oa[2], ob[2], queries), far_kv)
    oa.append(ring_z(oa[2]))
    ob.append(ring_x(ob[2]))
    info = jnp.concatenate([both, at.xl.astype(jnp.int32)[None]])
    info, half_b = lax.optimization_barrier((info, half_b))
    context = attend(info, queries, own_kv, far_kv)
    oa[3], ob[3] = after((oa[3], ob[3]), context)
    half_b = place_pair(half_b, 2, ob[2], ob[3], at)
    sums = []
    for part in range(2):
        other, mine = out_project(context, oa, half_b, 2 * part, at)
        sums.append((swap_core(other), mine))
    sums = [add_bf16(there, here).reshape(4, BLOCK, -1) for there, here in sums]
    attended = jnp.concatenate([scatter_sum(part, at.y, at.core) for part in sums], axis=1)
    return (attended,) + new_q + new_k + new_v + new_o


def solution(mesh):
    fine = Mesh(mesh.devices.reshape([SIZES[a] for a in AXES]), AXES)
    dp, tensor = ("z", "xh", "c"), ("y", "xl")
    weight = P(dp, tensor)
    rows = P(dp + tensor, None)
    return jax.shard_map(
        local,
        mesh=fine,
        in_specs=(rows, P(dp), P(), P(), P()) + (weight,) * 16,
        out_specs=(rows,) + (weight,) * 12,
        check_vma=False,
    )
```

```python
import functools
import itertools
import math

import jax
import jax.numpy as jnp
from jax import lax
from jax.experimental import pallas as pl
from jax.experimental.pallas import tpu as pltpu
from jax.sharding import Mesh
from jax.sharding import PartitionSpec as P

HEAD_SIZE = 128
STEP = 10

BETA_ONE = 0.9
BETA_TWO = 0.999
ADAM_EPS = 1e-08
LEARN_RATE = 0.0001
DECAY_RATE = 0.01
NORM_EPS = 1e-06
ROPE_BASE = 1000000.0

AXES = ("z", "xh", "c", "y", "xl")
SIZES = dict(z=4, xh=2, c=2, y=4, xl=2)
WIDTH = 5120
BLOCK = 128
OWN = 512
BF16 = jnp.bfloat16
F32 = jnp.float32


def adamw_step(current, moment, second, gradient):
    moment_new = BETA_ONE * moment + (1.0 - BETA_ONE) * gradient
    second_new = BETA_TWO * second + (1.0 - BETA_TWO) * gradient * gradient
    moment_hat = moment_new / (1.0 - BETA_ONE**STEP)
    second_hat = second_new / (1.0 - BETA_TWO**STEP)
    updated = current - LEARN_RATE * (
        moment_hat / (jnp.sqrt(second_hat) + ADAM_EPS) + DECAY_RATE * current
    )
    return (updated, moment_new, second_new)


def root_mean_scale(values, gain):
    mean_sq = jnp.mean(values * values, axis=-1, keepdims=True)
    return values * lax.rsqrt(mean_sq + NORM_EPS) * gain


def permute(axes, move):
    axes = tuple(a for a in AXES if a in axes)
    places = list(itertools.product(*[range(SIZES[a]) for a in axes]))
    index = {place: i for i, place in enumerate(places)}
    pairs = []
    for place in places:
        there = move(dict(zip(axes, place)))
        pairs.append((index[place], index[tuple(there[a] for a in axes)]))
    return lambda v: lax.ppermute(v, axes, pairs)


def ring_move(axis):
    def move(place):
        step = 1 if place["c"] == 0 else -1
        if axis == "x":
            x = (place["xh"] * 2 + place["xl"] + step) % 4
            place["xh"], place["xl"] = x // 2, x % 2
        else:
            place[axis] = (place[axis] + step) % SIZES[axis]
        return place

    return move


def swap_move(axis):
    def move(place):
        place[axis] = 1 - place[axis]
        return place

    return move


ring_y = permute(("y", "c"), ring_move("y"))
swap_xl = permute(("xl",), swap_move("xl"))


def position_tables(xl):
    block = jnp.arange(4, dtype=jnp.int32)[:, None] * 2 + xl
    places = (block * BLOCK + jnp.arange(BLOCK, dtype=jnp.int32)[None, :]).reshape(-1)
    freqs = ROPE_BASE ** (-jnp.arange(0, HEAD_SIZE, 2, dtype=F32) / HEAD_SIZE)
    angles = places.astype(F32)[:, None] * freqs[None, :]
    cosine, sine = jnp.cos(angles), jnp.sin(angles)
    return (
        jnp.concatenate([cosine, cosine], axis=-1),
        jnp.concatenate([-sine, sine], axis=-1),
    )


def norm_rope(u, gain, cosine, sine):
    mean_sq = jnp.mean(u * u, axis=-1, keepdims=True)
    u = u * lax.rsqrt(mean_sq + NORM_EPS) * gain
    return u * cosine + pltpu.roll(u, HEAD_SIZE // 2, 1) * sine


def qkv_kernel(x_ref, w_ref, cos_ref, sin_ref, qg_ref, kg_ref, q_ref, kv_ref, acc):
    step = pl.program_id(1)
    last = pl.num_programs(1) - 1
    rows = x_ref[...]
    for n in range(0, 1280, 256):
        part = w_ref[0, :, 0, :, :, n : n + 256].reshape(1280, 256)
        out = jnp.dot(rows, part, preferred_element_type=F32)

        @pl.when(step == 0)
        def _():
            acc[:, n : n + 256] = out

        @pl.when(step > 0)
        def _():
            acc[:, n : n + 256] += out

    @pl.when(step == last)
    def _():
        cosine, sine = cos_ref[...], sin_ref[...]
        for h in range(8):
            u = acc[:, h * 128 : (h + 1) * 128]
            q_ref[0, :, h * 128 : (h + 1) * 128] = norm_rope(u, qg_ref[...], cosine, sine).astype(BF16)
        kv_ref[0, :, :128] = norm_rope(acc[:, 1024:1152], kg_ref[...], cosine, sine).astype(BF16)
        kv_ref[0, :, 128:] = acc[:, 1152:1280].astype(BF16)


def qkv_project(rows, weights, cosine, sine, q_gain, k_gain):
    whole = lambda shape: pl.BlockSpec(shape, lambda g, s: (0,) * len(shape))
    return pl.pallas_call(
        qkv_kernel,
        grid=(2, 4),
        in_specs=[
            pl.BlockSpec((OWN, 1280), lambda g, s: (0, s)),
            pl.BlockSpec((1, 2, 1, 2, 320, 1280), lambda g, s: (s, 0, g, 0, 0, 0)),
            whole((OWN, 128)),
            whole((OWN, 128)),
            whole((1, 128)),
            whole((1, 128)),
        ],
        out_specs=[
            pl.BlockSpec((1, OWN, 1024), lambda g, s: (g, 0, 0)),
            pl.BlockSpec((1, OWN, 256), lambda g, s: (g, 0, 0)),
        ],
        out_shape=[
            jax.ShapeDtypeStruct((2, OWN, 1024), BF16),
            jax.ShapeDtypeStruct((2, OWN, 256), BF16),
        ],
        scratch_shapes=[pltpu.VMEM((OWN, 1280), F32)],
        compiler_params=pltpu.CompilerParams(vmem_limit_bytes=48 << 20),
        cost_estimate=pl.CostEstimate(flops=2 * 512 * 5120 * 2560, bytes_accessed=40 << 20, transcendentals=0),
        name="qkv",
    )(rows, weights, cosine, sine, q_gain, k_gain)


SCALE = math.log2(math.e) / math.sqrt(HEAD_SIZE)


def attend_kernel(info_ref, q_ref, own_ref, far_ref, o_ref):
    length, xl = info_ref[0], info_ref[1]
    block = pl.program_id(1)

    def body(j):
        n = (j + 1) * BLOCK
        keys = jnp.concatenate([own_ref[0, :n, :128], far_ref[0, :n, :128]], axis=0)
        values = jnp.concatenate([own_ref[0, :n, 128:], far_ref[0, :n, 128:]], axis=0)
        values = jnp.concatenate([values, jnp.ones_like(values)], axis=1)
        row = lax.broadcasted_iota(jnp.int32, (BLOCK, 2 * n), 0)
        col = lax.broadcasted_iota(jnp.int32, (BLOCK, 2 * n), 1)
        own = col < n
        inner = jnp.where(own, col, col - n)
        side = jnp.where(own, xl, 1 - xl)
        place = (inner // BLOCK * 2 + side) * BLOCK + inner % BLOCK
        query = (2 * j + xl) * BLOCK + row
        bias = jnp.where((place <= query) & (place < length), 0.0, -1e30).astype(F32)
        for h in range(8):
            lanes = slice(h * 128, (h + 1) * 128)
            scores = lax.dot_general(
                q_ref[0, :, lanes], keys, (((1,), (1,)), ((), ())), preferred_element_type=F32
            )
            scores = scores + bias
            top = jnp.max(scores, axis=-1, keepdims=True)
            exps = jnp.exp2((scores - top) * SCALE).astype(BF16)
            mixed = jnp.dot(exps, values, preferred_element_type=F32)
            o_ref[0, :, lanes] = (mixed[:, :128] / mixed[:, 128:]).astype(BF16)

    for j in range(4):
        pl.when(block == j)(functools.partial(body, j))


def attend(info, queries, own, far):
    return pl.pallas_call(
        attend_kernel,
        grid=(2, 4),
        in_specs=[
            pl.BlockSpec(memory_space=pltpu.SMEM),
            pl.BlockSpec((1, BLOCK, 1024), lambda g, j: (g, j, 0)),
            pl.BlockSpec((1, OWN, 256), lambda g, j: (g, 0, 0)),
            pl.BlockSpec((1, OWN, 256), lambda g, j: (g, 0, 0)),
        ],
        out_specs=pl.BlockSpec((1, BLOCK, 1024), lambda g, j: (g, j, 0)),
        out_shape=jax.ShapeDtypeStruct((2, OWN, 1024), BF16),
        compiler_params=pltpu.CompilerParams(vmem_limit_bytes=48 << 20),
        cost_estimate=pl.CostEstimate(flops=6 << 30, bytes_accessed=5 << 20, transcendentals=5 << 20),
        name="attend",
    )(info, queries, own, far)


def out_kernel(ctx_ref, w_ref, o_ref):
    for f in range(4):
        total = None
        for g in range(2):
            part = lax.dot_general(
                ctx_ref[g],
                w_ref[0, f // 2, g, f % 2],
                (((1,), (1,)), ((), ())),
                preferred_element_type=F32,
            )
            total = part if total is None else total + part
        o_ref[:, f * 320 : (f + 1) * 320] = total.astype(BF16)


def out_project(context, weights, first, count):
    return pl.pallas_call(
        out_kernel,
        grid=(count,),
        in_specs=[
            pl.BlockSpec((2, OWN, 1024), lambda s: (0, 0, 0)),
            pl.BlockSpec((1, 2, 2, 2, 320, 1024), lambda s: (s + first, 0, 0, 0, 0, 0)),
        ],
        out_specs=pl.BlockSpec((OWN, 1280), lambda s: (0, s)),
        out_shape=jax.ShapeDtypeStruct((OWN, 1280 * count), BF16),
        compiler_params=pltpu.CompilerParams(vmem_limit_bytes=48 << 20),
        cost_estimate=pl.CostEstimate(
            flops=2 * 512 * 2048 * 1280 * count, bytes_accessed=count * (7 << 20), transcendentals=0
        ),
        name="out_project",
    )(context, weights)


def scatter_sum(partial, y, core):
    blocks = partial.reshape(4, BLOCK, -1)
    step = 1 - 2 * core

    def own(back):
        return lax.dynamic_index_in_dim(blocks, jnp.mod(y - step * back, 4), 0, keepdims=False)

    moving = own(1)
    for s in range(1, 4):
        arrived = ring_y(moving)
        moving = (arrived.astype(F32) + own(s + 1).astype(F32)).astype(BF16)
    return moving


def gather_tokens(mine, y, core):
    step = 1 - 2 * core
    whole = jnp.zeros((4, BLOCK, WIDTH), BF16)
    moving = mine
    for s in range(4):
        whole = lax.dynamic_update_index_in_dim(whole, moving, jnp.mod(y - step * s, 4), 0)
        if s < 3:
            moving = ring_y(moving)
    return whole.reshape(OWN, WIDTH)


def after(value, *before):
    return lax.optimization_barrier((value,) + before)[0]


def gather_weights(shard):
    whole = lax.all_gather(shard, ("z", "xh", "xl", "c"), axis=0, tiled=False)
    return whole.reshape((4, 2, 2, 2) + shard.shape)


def local(
    tokens,
    lengths,
    attn_gain,
    q_gain,
    key_norm_gain,
    wq_param,
    wq_moment,
    wq_second,
    wq_grad,
    key_weight_matrix,
    key_weight_first_moment,
    key_weight_second_moment,
    key_weight_gradient,
    value_weight_matrix,
    value_weight_first_moment,
    value_weight_second_moment,
    value_weight_gradient,
    wo_param,
    wo_moment,
    wo_second,
    wo_grad,
):
    y, core, xl = lax.axis_index("y"), lax.axis_index("c"), lax.axis_index("xl")
    new_k = adamw_step(
        key_weight_matrix, key_weight_first_moment, key_weight_second_moment, key_weight_gradient
    )
    new_v = adamw_step(
        value_weight_matrix,
        value_weight_first_moment,
        value_weight_second_moment,
        value_weight_gradient,
    )
    new_q = adamw_step(wq_param, wq_moment, wq_second, wq_grad)
    shard_qkv = jnp.concatenate([new_q[0], new_k[0], new_v[0]], axis=1).astype(BF16)
    whole_qkv = gather_weights(shard_qkv)
    wo_grad, tokens = after((wo_grad, tokens), shard_qkv)
    new_o = adamw_step(wo_param, wo_moment, wo_second, wo_grad)
    shard_o = new_o[0].astype(BF16)
    normed_own = root_mean_scale(tokens.astype(F32), attn_gain).astype(BF16)
    whole_o = gather_weights(shard_o)
    normed = gather_tokens(normed_own, y, core)
    cosine, sine = position_tables(xl)
    queries, own_kv = qkv_project(
        normed, whole_qkv, cosine, sine, q_gain[None], key_norm_gain[None]
    )
    far_kv = swap_xl(own_kv)
    info = jnp.stack([lengths[0], xl.astype(jnp.int32)])
    context = attend(info, queries, own_kv, far_kv)
    halves = [
        scatter_sum(out_project(context, whole_o, first, count), y, core)
        for first, count in ((0, 2), (2, 2))
    ]
    attended = jnp.concatenate(halves, axis=1)
    return (attended,) + new_q + new_k + new_v + new_o


def solution(mesh):
    fine = Mesh(mesh.devices.reshape([SIZES[a] for a in AXES]), AXES)
    dp, tensor = ("z", "xh", "c"), ("y", "xl")
    weight = P(dp, tensor)
    rows = P(dp + tensor, None)
    return jax.shard_map(
        local,
        mesh=fine,
        in_specs=(rows, P(dp), P(), P(), P()) + (weight,) * 16,
        out_specs=(rows,) + (weight,) * 12,
        check_vma=False,
    )
```
